128 devices in a mesh: row: 8 (over z, core), col: 16 (over x, y).
Axes of the slice: x: 4, y: 4, z: 4, core: 2. Of those that a mesh axis runs over, the one named last changes fastest.
Arguments:
- leaf_rhs: bfloat16 [6144, 512, 128], P(('row', 'col')), may hold values from -6 to 6
- leaf_inv: bfloat16 [6144, 128, 128], P(('row', 'col')), as said below
- leaf_off: bfloat16 [6144, 3, 128, 128], P(('row', 'col')), may hold values from -0.0234375 to 0.0234375
- blocks: int32 [6144, 3], P(('row', 'col')), may hold values from 0 to 31, all different within a row
- par_rhs: bfloat16 [32, 512, 128], P('col', 'row'), may hold values from -6 to 6
- par_inv: bfloat16 [32, 128, 128], P('col', 'row'), as said below
Outputs:
- leaf_x: bfloat16 [6144, 512, 128], P(('row', 'col'))
- par_x: bfloat16 [32, 512, 128], P('col', 'row')
The draws below stay inside these ranges and needn't reach their ends.
Inputs may be any that keep to these rules, and one draw needn't show every extreme that they name: `blocks`: each row names 3 different parent supernodes, and every parent supernode is named by some row. `leaf_inv`: each block is lower triangular with a diagonal between 0.8 and 1.25. `par_inv`: each block is lower triangular with a diagonal between 0.8 and 1.25.
All inputs are finite; a program needn't handle non-finite values.
Results may differ from the reference program's by a relative error of at most 0.0053.
Values may be sent and summed in bfloat16 or wider, within the bound.
No kernel may reach another device: no remote copies, remote signals or barrier semaphores. Data moves between devices by JAX's collectives and lax.ppermute only.
A program may use at most 192 MiB of HBM per device.

```python
import math
import jax
import jax.numpy as jnp
from jax import lax

B = 128
NRHS = 512
K = 3
LEAF_DEV = 48
NLEAF = 6144
NPAR = 32
DEVICES = 128


def draw_triangular(key, total):
    first_key = jax.random.fold_in(key, 11)
    second_key = jax.random.fold_in(key, 23)
    beneath = jax.random.normal(first_key, (total, B, B), jnp.float32) * (0.6 / math.sqrt(B))
    diagonal = jax.random.uniform(second_key, (total, B), jnp.float32, 0.8, 1.25)
    row_ids = lax.broadcasted_iota(jnp.int32, (B, B), 0)
    col_ids = lax.broadcasted_iota(jnp.int32, (B, B), 1)
    lower_mask = (row_ids > col_ids).astype(jnp.float32)
    identity = (row_ids == col_ids).astype(jnp.float32)
    return (beneath * lower_mask + identity * diagonal[:, :, None]).astype(jnp.bfloat16)


def draw_leaf_inv(key, part):
    return draw_triangular(key, NLEAF)


def draw_par_inv(key, part):
    return draw_triangular(key, NPAR)


def level_of(own_key, extent, split, smallest, high):
    def one(position, parts):
        heights = jax.random.uniform(jax.random.fold_in(jax.random.fold_in(own_key, 6), position), (parts,), jnp.float32, smallest / len(split), high / len(split))
        return jnp.repeat(jnp.exp(heights), extent[position] // parts).reshape((-1,) + (1,) * (len(extent) - position - 1))

    factor_of = one(*split[0])
    for cut in split[1:]:
        factor_of = factor_of * one(*cut)
    return factor_of


def distinct(own_key, rows, amount, top, lift):
    order = jax.random.permutation(jax.random.fold_in(own_key, 1), amount)
    pull = order
    for power in range(3):
        pull = pull * pull // amount
    pull = pull * lift // amount
    chance = jax.random.randint(jax.random.fold_in(own_key, 2), (rows, amount), 0, 4096) + pull
    fixed_rows = jax.random.permutation(jax.random.fold_in(own_key, 3), rows)[jnp.arange(amount) % rows]
    chance = jnp.where(jnp.arange(rows)[:, None] == fixed_rows[None, :], 1 << 14, chance)
    merit = chance * amount + jnp.arange(amount)
    return lax.top_k(merit.astype(jnp.int32), top)[1].astype(jnp.int32)


def scatter_about(rng, dims, width, bound, split=(), dtype=jnp.bfloat16):
    gain = level_of(rng, dims, split, -0.22, 0.18) if split else 1.0
    values = jax.random.normal(rng, dims, jnp.float32) * width * gain
    return jnp.minimum(jnp.maximum(values, -bound), bound).astype(dtype)


def setup_inputs(seed: int = 0) -> dict:
    streams_of = jax.random.split(jax.random.key(seed), 7)
    return {
        "leaf_rhs": scatter_about(streams_of[0], (NLEAF, NRHS, B), 1.0, 6.0, ((0, 128),)),
        "leaf_inv": draw_leaf_inv(jax.random.fold_in(streams_of[6], 71), 0),
        "leaf_off": scatter_about(streams_of[2], (NLEAF, K, B, B), (B * LEAF_DEV * DEVICES * K // NPAR) ** -0.5, 0.0234375, ((0, 128),)),
        "blocks": distinct(streams_of[3], NLEAF, NPAR, K, 1536),
        "par_rhs": scatter_about(streams_of[4], (NPAR, NRHS, B), 1.0, 6.0, ((0, 16), (1, 8))),
        "par_inv": draw_par_inv(jax.random.fold_in(streams_of[6], 71), 0),
    }


def reference(leaf_rhs, leaf_inv, leaf_off, blocks, par_rhs, par_inv):
    groups = NLEAF // LEAF_DEV
    highest = lax.Precision.HIGHEST
    rhs_groups = leaf_rhs.reshape(groups, LEAF_DEV, NRHS, B)
    inv_groups = leaf_inv.reshape(groups, LEAF_DEV, B, B)
    off_groups = leaf_off.reshape(groups, LEAF_DEV, K, B, B)
    id_groups = blocks.reshape(groups, LEAF_DEV, K)

    def forward(carry, item):
        given, inverse, offdiag, parent_ids = item
        solved = jnp.einsum('jrc,jbc->jrb', given.astype(jnp.float32), inverse.astype(jnp.float32), precision=highest).astype(jnp.bfloat16)
        contrib = jnp.einsum('jrb,jkcb->jkrc', solved.astype(jnp.float32), offdiag.astype(jnp.float32), precision=highest)
        carry = carry + jax.ops.segment_sum(contrib.reshape(LEAF_DEV * K, NRHS, B), parent_ids.reshape(LEAF_DEV * K), num_segments=NPAR)
        return carry, solved

    start_sum = jnp.zeros((NPAR, NRHS, B), jnp.float32)
    updates, leaf_y = lax.scan(forward, start_sum, (rhs_groups, inv_groups, off_groups, id_groups))
    remainder = par_rhs.astype(jnp.float32) - updates
    par_y = jnp.einsum('prc,pbc->prb', remainder, par_inv.astype(jnp.float32), precision=highest).astype(jnp.bfloat16)
    par_x = jnp.einsum('prb,pbc->prc', par_y.astype(jnp.float32), par_inv.astype(jnp.float32), precision=highest).astype(jnp.bfloat16)

    def backward(item):
        solved, inverse, offdiag, parent_ids = item
        chosen = jnp.take(par_x, parent_ids.reshape(-1), axis=0).reshape(LEAF_DEV, K, NRHS, B)
        back = jnp.einsum('jkrc,jkcb->jrb', chosen.astype(jnp.float32), offdiag.astype(jnp.float32), precision=highest)
        return jnp.einsum('jrb,jbc->jrc', solved.astype(jnp.float32) - back, inverse.astype(jnp.float32), precision=highest).astype(jnp.bfloat16)

    leaf_x = lax.map(backward, (leaf_y, inv_groups, off_groups, id_groups))
    return leaf_x.reshape(NLEAF, NRHS, B), par_x
```

```python
import functools

import jax
import jax.numpy as jnp
from jax import lax
from jax.experimental import pallas as pl
from jax.experimental.pallas import tpu as pltpu
from jax.sharding import PartitionSpec as P

F32, BF16 = jnp.float32, jnp.bfloat16
VMEM_LIMIT = 56 * 1024 * 1024
CORES = 2


def params(n=1):
    return pltpu.CompilerParams(
        vmem_limit_bytes=VMEM_LIMIT, dimension_semantics=("arbitrary",) * n
    )


def mm_t(a, b):
    return lax.dot_general(a, b, (((1,), (1,)), ((), ())), preferred_element_type=F32)


def mm(a, b):
    return jnp.dot(a, b, preferred_element_type=F32)


def forward_kernel(step_leaves, fanout, heights, blocks, core, rhs, inv, off, y_out, keep, send, acc):
    step = pl.program_id(0)
    parents, block_rows, width = acc.shape[2:]

    @pl.when(step == 0)
    def _():
        acc[...] = jnp.zeros_like(acc)

    for i in range(step_leaves):
        y = mm_t(rhs[i], inv[i]).astype(BF16)
        y_out[i] = y
        for k in range(fanout):
            parent = blocks[(step * step_leaves + i) * fanout + k]
            part = mm_t(y, off[i, k])
            for z in range(heights):
                for c in range(CORES):
                    at = (z * CORES + c) * block_rows
                    acc[c, z, parent] += part[at : at + block_rows]

    @pl.when(step == pl.num_programs(0) - 1)
    def _():
        me = core[0]
        keep[...] = acc[me]
        send[...] = acc[1 - me].astype(BF16)


def forward(blocks, core, rhs, inv, off, parents, rows):
    leaves, nrhs, width = rhs.shape
    fanout = off.shape[1]
    heights = rows // CORES
    block_rows = nrhs // rows
    g = 4
    half = (heights, parents, block_rows, width)
    return pl.pallas_call(
        functools.partial(forward_kernel, g, fanout, heights),
        grid_spec=pltpu.PrefetchScalarGridSpec(
            num_scalar_prefetch=2,
            grid=(leaves // g,),
            in_specs=[
                pl.BlockSpec((g, nrhs, width), lambda s, *_: (s, 0, 0)),
                pl.BlockSpec((g, width, width), lambda s, *_: (s, 0, 0)),
                pl.BlockSpec((g, fanout, width, width), lambda s, *_: (s, 0, 0, 0)),
            ],
            out_specs=[
                pl.BlockSpec((g, nrhs, width), lambda s, *_: (s, 0, 0)),
                pl.BlockSpec(half, lambda s, *_: (0, 0, 0, 0)),
                pl.BlockSpec(half, lambda s, *_: (0, 0, 0, 0)),
            ],
            scratch_shapes=[pltpu.VMEM((CORES,) + half, F32)],
        ),
        out_shape=[
            jax.ShapeDtypeStruct(rhs.shape, BF16),
            jax.ShapeDtypeStruct(half, F32),
            jax.ShapeDtypeStruct(half, BF16),
        ],
        compiler_params=params(),
        name="forward",
        cost_estimate=pl.CostEstimate(
            flops=2 * leaves * nrhs * width * width * (1 + fanout),
            bytes_accessed=26_000_000,
            transcendentals=0,
        ),
    )(blocks, core, rhs, inv, off)


def fold_kernel(step_leaves, fanout, inv, off, out):
    for i in range(step_leaves):
        for k in range(fanout):
            out[i, k] = mm(off[i, k], inv[i]).astype(BF16)


def fold(inv, off):
    leaves, fanout, width, _ = off.shape
    g = 8
    return pl.pallas_call(
        functools.partial(fold_kernel, g, fanout),
        grid=(leaves // g,),
        in_specs=[
            pl.BlockSpec((g, width, width), lambda s: (s, 0, 0)),
            pl.BlockSpec((g, fanout, width, width), lambda s: (s, 0, 0, 0)),
        ],
        out_specs=pl.BlockSpec((g, fanout, width, width), lambda s: (s, 0, 0, 0)),
        out_shape=jax.ShapeDtypeStruct(off.shape, BF16),
        compiler_params=params(),
        name="fold",
        cost_estimate=pl.CostEstimate(
            flops=2 * leaves * fanout * width**3,
            bytes_accessed=11_000_000,
            transcendentals=0,
        ),
    )(inv, off)


def parent_kernel(sources, got, rhs, inv, x_out, x_every):
    own, block_rows, width = rhs.shape
    total = got[0].astype(F32)
    for s in range(1, sources):
        total += got[s].astype(F32)
    for p in range(own):
        rest = rhs[p].astype(F32) - total[p]
        high = rest.astype(BF16)
        left = rest - high.astype(F32)
        mid = left.astype(BF16)
        low = (left - mid.astype(F32)).astype(BF16)
        w = inv[p]
        y = (mm_t(low, w) + mm_t(mid, w)) + mm_t(high, w)
        x = mm(y.astype(BF16), w).astype(BF16)
        x_out[p] = x
        for s in range(sources):
            x_every[s, p] = x


def parent(got, rhs, inv):
    sources = got.shape[0]
    return pl.pallas_call(
        functools.partial(parent_kernel, sources),
        out_shape=[
            jax.ShapeDtypeStruct(rhs.shape, BF16),
            jax.ShapeDtypeStruct(got.shape, BF16),
        ],
        compiler_params=params(0),
        name="parent",
        cost_estimate=pl.CostEstimate(
            flops=30_000_000, bytes_accessed=4_500_000, transcendentals=0
        ),
    )(got, rhs, inv)


def backward_kernel(step_leaves, fanout, heights, blocks, core, y, inv, folded, mine, other, out, xs, lhs):
    step = pl.program_id(0)
    block_rows, width = mine.shape[2:]

    @pl.when(step == 0)
    def _():
        me = core[0]
        xs[me] = mine[...]
        xs[1 - me] = other[...]

    for i in range(step_leaves):
        for k in range(fanout):
            p = blocks[(step * step_leaves + i) * fanout + k]
            for z in range(heights):
                for c in range(CORES):
                    at = (z * CORES + c) * block_rows
                    lhs[i, at : at + block_rows, k * width : (k + 1) * width] = xs[c, z, p]
        back = mm(lhs[i], folded[i].reshape(fanout * width, width))
        out[i] = (mm(y[i], inv[i]) - back).astype(BF16)


def backward(blocks, core, y, inv, folded, mine, other):
    leaves, nrhs, width = y.shape
    fanout = folded.shape[1]
    heights = mine.shape[0]
    g = 4
    return pl.pallas_call(
        functools.partial(backward_kernel, g, fanout, heights),
        grid_spec=pltpu.PrefetchScalarGridSpec(
            num_scalar_prefetch=2,
            grid=(leaves // g,),
            in_specs=[
                pl.BlockSpec((g, nrhs, width), lambda s, *_: (s, 0, 0)),
                pl.BlockSpec((g, width, width), lambda s, *_: (s, 0, 0)),
                pl.BlockSpec((g, fanout, width, width), lambda s, *_: (s, 0, 0, 0)),
                pl.BlockSpec(mine.shape, lambda s, *_: (0, 0, 0, 0)),
                pl.BlockSpec(mine.shape, lambda s, *_: (0, 0, 0, 0)),
            ],
            out_specs=pl.BlockSpec((g, nrhs, width), lambda s, *_: (s, 0, 0)),
            scratch_shapes=[
                pltpu.VMEM((CORES,) + mine.shape, BF16),
                pltpu.VMEM((g, nrhs, fanout * width), BF16),
            ],
        ),
        out_shape=jax.ShapeDtypeStruct(y.shape, BF16),
        compiler_params=params(),
        name="backward",
        cost_estimate=pl.CostEstimate(
            flops=2 * leaves * nrhs * width * width * (1 + fanout),
            bytes_accessed=23_000_000,
            transcendentals=0,
        ),
    )(blocks, core, y, inv, folded, mine, other)


def gather_inverse(par_inv, rows):
    own, part, width = par_inv.shape
    heights = rows // CORES
    place = lax.axis_index("row")
    across = lax.ppermute(par_inv, "row", [(r, r ^ 1) for r in range(rows)])
    pair = jnp.where(
        place % CORES == 0, jnp.stack([par_inv, across]), jnp.stack([across, par_inv])
    )
    parts = [pair] + [
        lax.ppermute(pair, "row", [(r, (r + CORES * s) % rows) for r in range(rows)])
        for s in range(1, heights)
    ]
    z = place // CORES
    stacked = jnp.stack(parts)
    whole = jnp.zeros_like(stacked)
    for h in range(heights):
        pick = sum(
            jnp.where((z - h) % heights == s, parts[s].astype(F32), 0.0) for s in range(heights)
        )
        whole = whole.at[h].set(pick.astype(BF16))
    return whole.transpose(2, 0, 1, 3, 4).reshape(own, rows * part, width)


def on_device(rows, cols, leaf_rhs, leaf_inv, leaf_off, blocks, par_rhs, par_inv):
    own, block_rows, width = par_rhs.shape
    parents = own * cols
    heights = rows // CORES
    chips = heights * cols
    core = (lax.axis_index("row") % CORES).astype(jnp.int32).reshape(1)
    flat = blocks.reshape(-1)
    swap = [(r, r ^ 1) for r in range(rows)]
    groups = [
        [(z * CORES + c) * cols + k for z in range(heights) for k in range(cols)]
        for c in range(CORES)
    ]
    spread = functools.partial(
        lax.all_to_all,
        axis_name=("row", "col"),
        split_axis=0,
        concat_axis=0,
        axis_index_groups=groups,
        tiled=True,
    )

    inverse = gather_inverse(par_inv, rows)
    leaf_y, keep, send = forward(flat, core, leaf_rhs, leaf_inv, leaf_off, parents, rows)
    chip = (keep + lax.ppermute(send, "row", swap).astype(F32)).astype(BF16)
    got = spread(chip.reshape(chips, own, block_rows, width))
    folded = fold(leaf_inv, leaf_off)
    par_x, every = parent(got, par_rhs, inverse)
    mine = spread(every).reshape(heights, parents, block_rows, width)
    other = lax.ppermute(mine, "row", swap)
    leaf_x = backward(flat, core, leaf_y, leaf_inv, folded, mine, other)
    return (leaf_x, par_x)


def solution(mesh):
    rows, cols = mesh.shape["row"], mesh.shape["col"]
    return jax.shard_map(
        functools.partial(on_device, rows, cols),
        mesh=mesh,
        in_specs=(
            P(("row", "col"), None, None),
            P(("row", "col"), None, None),
            P(("row", "col"), None, None, None),
            P(("row", "col"), None),
            P("col", "row", None),
            P("col", "row", None),
        ),
        out_specs=(P(("row", "col"), None, None), P("col", "row", None)),
        check_vma=False,
    )
```

```python
import functools

import jax
import jax.numpy as jnp
from jax import lax
from jax.experimental import pallas as pl
from jax.experimental.pallas import tpu as pltpu
from jax.sharding import PartitionSpec as P

F32, BF16 = jnp.float32, jnp.bfloat16
F_G, F_S, B_G, B_S = 12, 2, 12, 2
CORES = 2


def params(mib):
    return pltpu.CompilerParams(vmem_limit_bytes=mib * 1024 * 1024)


def in_hbm(*arrays):
    return [pltpu.with_memory_space_constraint(a, pltpu.HBM) for a in arrays]


def cost(flops, moved):
    return pl.CostEstimate(flops=flops, bytes_accessed=moved, transcendentals=0)


def mm_t(a, b):
    return lax.dot_general(a, b, (((1,), (1,)), ((), ())), preferred_element_type=F32)


def mm(a, b):
    return jnp.dot(a, b, preferred_element_type=F32)


def diagonal(ref, slot, blocks):
    row = col = 0
    for b in blocks:
        ref[slot, row : row + b.shape[0], col : col + b.shape[1]] = b
        row, col = row + b.shape[0], col + b.shape[1]


def forward_kernel(
    g, fanout, blocks, core, rhs_hbm, inv_hbm, off_hbm, keep_hbm, send_hbm,
    rhs, inv, off, acc, staged, w_inv, w_off, in_sems, out_sems,
):
    leaves = rhs.shape[0]
    _, heights, parents, block_rows, width = acc.shape
    half = heights * block_rows
    me = core[0]

    def fetches(i):
        some = pl.ds(g * i, g)
        return [
            pltpu.make_async_copy(hbm.at[some], vmem.at[some], in_sems.at[n, i])
            for n, (hbm, vmem) in enumerate(((inv_hbm, inv), (rhs_hbm, rhs), (off_hbm, off)))
        ]

    for i in range(leaves // g):
        for copy in fetches(i):
            copy.start()

    w_inv[...] = jnp.zeros_like(w_inv)
    w_off[...] = jnp.zeros_like(w_off)
    acc[...] = jnp.zeros_like(acc)

    def pair(j, slot):
        diagonal(w_inv, slot, [inv[j], inv[j + 1]])
        diagonal(w_off, slot, [off[j + h].reshape(fanout * width, width) for h in range(2)])
        x = jnp.concatenate(
            [
                jnp.concatenate(
                    [rhs[j + h, z, c] for c in (me, 1 - me) for z in range(heights)], axis=0
                )
                for h in range(2)
            ],
            axis=1,
        )
        y = mm_t(x, w_inv[slot]).astype(BF16)
        part = mm_t(y, w_off[slot])
        for h in range(2):
            for k in range(fanout):
                p = blocks[(j + h) * fanout + k]
                at = (h * fanout + k) * width
                for c in range(CORES):
                    for z in range(heights):
                        row = c * half + z * block_rows
                        acc[c, z, p] += part[row : row + block_rows, at : at + width]

    @pl.loop(0, leaves // g)
    def _(i):
        for copy in fetches(i):
            copy.wait()
        for u in range(0, g, 2):
            pair(i * g + u, (u // 2) % w_inv.shape[0])

    copies = []
    for z in range(heights):
        for c, out in ((1, send_hbm), (0, keep_hbm)):
            staged[c, z] = acc[c, z].astype(BF16)
            copies.append(pltpu.make_async_copy(staged.at[c, z], out.at[z], out_sems.at[c, z]))
            copies[-1].start()
    for copy in copies:
        copy.wait()


def forward(blocks, core, rhs, inv, off, parents):
    leaves, heights, _, block_rows, width = rhs.shape
    fanout = off.shape[1]
    half = (heights, parents, block_rows, width)
    g, slots = F_G, F_S
    smem, hbm = pl.BlockSpec(memory_space=pltpu.SMEM), pl.BlockSpec(memory_space=pltpu.HBM)
    return pl.pallas_call(
        functools.partial(forward_kernel, g, fanout),
        in_specs=[smem, smem, hbm, hbm, hbm],
        out_specs=[hbm, hbm],
        scratch_shapes=[
            pltpu.VMEM(rhs.shape, BF16),
            pltpu.VMEM(inv.shape, BF16),
            pltpu.VMEM(off.shape, BF16),
            pltpu.VMEM((CORES,) + half, F32),
            pltpu.VMEM((CORES,) + half, BF16),
            pltpu.VMEM((slots, 2 * width, 2 * width), BF16),
            pltpu.VMEM((slots, 2 * fanout * width, 2 * width), BF16),
            pltpu.SemaphoreType.DMA((3, leaves // g)),
            pltpu.SemaphoreType.DMA((CORES, heights)),
        ],
        out_shape=[jax.ShapeDtypeStruct(half, BF16)] * 2,
        compiler_params=params(48),
        name="forward",
        cost_estimate=cost(7_000_000_000, 19_000_000),
    )(blocks, core, *in_hbm(rhs, inv, off))


def fold_kernel(g, fanout, inv, off, out, w_inv):
    width = inv.shape[-1]

    @pl.when(pl.program_id(0) == 0)
    def _():
        w_inv[...] = jnp.zeros_like(w_inv)

    for i in range(0, g, 2):
        slot = (i // 2) % 2
        diagonal(w_inv, slot, [inv[i], inv[i + 1]])
        x = jnp.concatenate([off[i + h].reshape(fanout * width, width) for h in range(2)], axis=1)
        m = mm(x, w_inv[slot]).astype(BF16)
        for h in range(2):
            out[i + h] = m[:, h * width : (h + 1) * width]


def fold(inv, off):
    leaves, fanout, width, _ = off.shape
    g = 8
    return pl.pallas_call(
        functools.partial(fold_kernel, g, fanout),
        grid=(leaves // g,),
        in_specs=[
            pl.BlockSpec((g, width, width), lambda s: (s, 0, 0)),
            pl.BlockSpec((g, fanout, width, width), lambda s: (s, 0, 0, 0)),
        ],
        out_specs=pl.BlockSpec((g, fanout * width, width), lambda s: (s, 0, 0)),
        out_shape=jax.ShapeDtypeStruct((leaves, fanout * width, width), BF16),
        scratch_shapes=[pltpu.VMEM((2, 2 * width, 2 * width), BF16)],
        compiler_params=params(10),
        name="fold",
        cost_estimate=cost(4_000_000_000, 15_000_000),
    )(inv, off)


def leaf_kernel(g, rhs, inv, after, out, w_inv):
    width = inv.shape[-1]

    @pl.when(pl.program_id(0) == 0)
    def _():
        w_inv[...] = jnp.zeros_like(w_inv)

    for i in range(0, g, 2):
        slot = (i // 2) % 2
        diagonal(w_inv, slot, [inv[i], inv[i + 1]])
        x = jnp.concatenate([rhs[i], rhs[i + 1]], axis=1)
        y = mm_t(x, w_inv[slot]).astype(BF16)
        z = mm(y, w_inv[slot]).astype(BF16)
        for h in range(2):
            out[i + h] = z[:, h * width : (h + 1) * width]


def leaf(rhs, inv, after):
    leaves, nrhs, width = rhs.shape
    g = 8
    return pl.pallas_call(
        functools.partial(leaf_kernel, g),
        grid=(leaves // g,),
        in_specs=[
            pl.BlockSpec((g, nrhs, width), lambda s: (s, 0, 0)),
            pl.BlockSpec((g, width, width), lambda s: (s, 0, 0)),
            pl.BlockSpec(memory_space=pl.ANY),
        ],
        out_specs=pl.BlockSpec((g, nrhs, width), lambda s: (s, 0, 0)),
        out_shape=jax.ShapeDtypeStruct(rhs.shape, BF16),
        scratch_shapes=[pltpu.VMEM((2, 2 * width, 2 * width), BF16)],
        compiler_params=params(10),
        name="leaf",
        cost_estimate=cost(6_000_000_000, 20_000_000),
    )(rhs, inv, after)


def parent_kernel(sources, got, rhs, inv, after, x_out, x_every):
    own, block_rows, width = rhs.shape
    total = got[0].astype(F32)
    for s in range(1, sources):
        total += got[s].astype(F32)
    for p in range(own):
        rest = rhs[p].astype(F32) - total[p]
        high = rest.astype(BF16)
        left = rest - high.astype(F32)
        mid = left.astype(BF16)
        low = (left - mid.astype(F32)).astype(BF16)
        w = inv[p]
        y = (mm_t(low, w) + mm_t(mid, w)) + mm_t(high, w)
        x = mm(y.astype(BF16), w).astype(BF16)
        x_out[p] = x
        for s in range(sources):
            x_every[s, p] = x


def parent(got, rhs, inv, after):
    sources = got.shape[0]
    return pl.pallas_call(
        functools.partial(parent_kernel, sources),
        in_specs=[pl.BlockSpec(memory_space=pltpu.VMEM)] * 3 + [pl.BlockSpec(memory_space=pl.ANY)],
        out_shape=[
            jax.ShapeDtypeStruct(rhs.shape, BF16),
            jax.ShapeDtypeStruct(got.shape, BF16),
        ],
        compiler_params=params(16),
        name="parent",
        cost_estimate=cost(30_000_000, 4_500_000),
    )(got, rhs, inv, after)


def backward_kernel(g, fanout, blocks, which, base_hbm, folded_hbm, xs, *rest):
    out_hbm, base, folded, out, w, in_sems, out_sems = rest[-7:]
    leaves, heights, block_rows, width = base.shape
    c = which[0]

    def fetches(i):
        some = pl.ds(g * i, g)
        return [
            pltpu.make_async_copy(folded_hbm.at[some], folded.at[some], in_sems.at[0, i]),
            pltpu.make_async_copy(base_hbm.at[some, :, c], base.at[some], in_sems.at[1, i]),
        ]

    def store(i):
        some = pl.ds(g * i, g)
        return pltpu.make_async_copy(out.at[some], out_hbm.at[some, :, c], out_sems.at[i])

    for i in range(leaves // g):
        for copy in fetches(i):
            copy.start()

    w[...] = jnp.zeros_like(w)

    def pair(j, slot):
        diagonal(w, slot, [folded[j], folded[j + 1]])
        x = jnp.concatenate(
            [
                jnp.concatenate(
                    [xs[z, blocks[(j + h) * fanout + k]] for z in range(heights)], axis=0
                )
                for h in range(2)
                for k in range(fanout)
            ],
            axis=1,
        )
        back = mm(x, w[slot])
        for h in range(2):
            for z in range(heights):
                row = z * block_rows
                part = back[row : row + block_rows, h * width : (h + 1) * width]
                out[j + h, z] = (base[j + h, z].astype(F32) - part).astype(BF16)

    @pl.loop(0, leaves // g)
    def _(i):
        for copy in fetches(i):
            copy.wait()
        for u in range(0, g, 2):
            pair(i * g + u, (u // 2) % w.shape[0])
        store(i).start()

    for i in range(leaves // g):
        store(i).wait()


def backward(blocks, which, base, folded, xs, so_far=None):
    leaves, heights, _, block_rows, width = base.shape
    fanout = folded.shape[1] // width
    half = (leaves, heights, block_rows, width)
    g, slots = B_G, B_S
    more = [] if so_far is None else [so_far]
    smem, hbm = pl.BlockSpec(memory_space=pltpu.SMEM), pl.BlockSpec(memory_space=pltpu.HBM)
    return pl.pallas_call(
        functools.partial(backward_kernel, g, fanout),
        in_specs=[smem, smem, hbm, hbm, pl.BlockSpec(memory_space=pltpu.VMEM)] + [hbm] * len(more),
        out_specs=hbm,
        scratch_shapes=[
            pltpu.VMEM(half, BF16),
            pltpu.VMEM(folded.shape, BF16),
            pltpu.VMEM(half, BF16),
            pltpu.VMEM((slots, 2 * fanout * width, 2 * width), BF16),
            pltpu.SemaphoreType.DMA((2, leaves // g)),
            pltpu.SemaphoreType.DMA((leaves // g,)),
        ],
        out_shape=jax.ShapeDtypeStruct(base.shape, BF16),
        input_output_aliases={5: 0} if more else {},
        compiler_params=params(24),
        name="backward",
        cost_estimate=cost(5_000_000_000, 13_000_000),
    )(blocks, which, *in_hbm(base, folded), xs, *more)


def gather_inverse(par_inv, rows):
    own, part, width = par_inv.shape
    heights = rows // CORES
    place = lax.axis_index("row")
    across = lax.ppermute(par_inv, "row", [(r, r ^ 1) for r in range(rows)])
    pair = jnp.where(
        place % CORES == 0, jnp.stack([par_inv, across]), jnp.stack([across, par_inv])
    )
    parts = [pair] + [
        lax.ppermute(pair, "row", [(r, (r + CORES * s) % rows) for r in range(rows)])
        for s in range(1, heights)
    ]
    z = place // CORES
    stacked = jnp.stack(parts)
    whole = jnp.zeros_like(stacked)
    for h in range(heights):
        pick = sum(
            jnp.where((z - h) % heights == s, parts[s].astype(F32), 0.0) for s in range(heights)
        )
        whole = whole.at[h].set(pick.astype(BF16))
    return whole.transpose(2, 0, 1, 3, 4).reshape(own, rows * part, width)


def on_device(rows, cols, leaf_rhs, leaf_inv, leaf_off, blocks, par_rhs, par_inv):
    own, block_rows, width = par_rhs.shape
    parents = own * cols
    heights = rows // CORES
    chips = heights * cols
    core = (lax.axis_index("row") % CORES).astype(jnp.int32).reshape(1)
    flat = blocks.reshape(-1)
    swap = [(r, r ^ 1) for r in range(rows)]
    groups = [
        [(z * CORES + c) * cols + k for z in range(heights) for k in range(cols)]
        for c in range(CORES)
    ]
    spread = functools.partial(
        lax.all_to_all,
        axis_name=("row", "col"),
        split_axis=0,
        concat_axis=0,
        axis_index_groups=groups,
        tiled=True,
    )

    inverse = gather_inverse(par_inv, rows)
    by_core = (leaf_rhs.shape[0], heights, CORES, block_rows, width)
    keep, send = forward(flat, core, leaf_rhs.reshape(by_core), leaf_inv, leaf_off, parents)
    chip = (keep.astype(F32) + lax.ppermute(send, "row", swap).astype(F32)).astype(BF16)
    got = spread(chip.reshape(chips, own, block_rows, width))
    folded = fold(leaf_inv, leaf_off)
    par_x, every = parent(got, par_rhs, inverse, folded[0, :16])
    mine = spread(every).reshape(heights, parents, block_rows, width)
    base = leaf(leaf_rhs, leaf_inv, par_x).reshape(by_core)
    mine, base = lax.optimization_barrier((mine, base))
    other = lax.ppermute(mine, "row", swap)
    half = backward(flat, core, base, folded, mine)
    leaf_x = backward(flat, 1 - core, base, folded, other, half)
    return (leaf_x.reshape(leaf_rhs.shape), par_x)


def solution(mesh):
    rows, cols = mesh.shape["row"], mesh.shape["col"]
    return jax.shard_map(
        functools.partial(on_device, rows, cols),
        mesh=mesh,
        in_specs=(
            P(("row", "col"), None, None),
            P(("row", "col"), None, None),
            P(("row", "col"), None, None, None),
            P(("row", "col"), None),
            P("col", "row", None),
            P("col", "row", None),
        ),
        out_specs=(P(("row", "col"), None, None), P("col", "row", None)),
        check_vma=False,
    )
```

```python
import functools

import jax
import jax.numpy as jnp
from jax import lax
from jax.experimental import pallas as pl
from jax.experimental.pallas import tpu as pltpu
from jax.sharding import PartitionSpec as P

F32, BF16 = jnp.float32, jnp.bfloat16
F_G, F_S, B_G, B_S = 12, 2, 12, 2
CORES = 2


def params(mib):
    return pltpu.CompilerParams(vmem_limit_bytes=mib * 1024 * 1024)


def in_hbm(*arrays):
    return [pltpu.with_memory_space_constraint(a, pltpu.HBM) for a in arrays]


def cost(flops, moved):
    return pl.CostEstimate(flops=flops, bytes_accessed=moved, transcendentals=0)


def mm_t(a, b):
    return lax.dot_general(a, b, (((1,), (1,)), ((), ())), preferred_element_type=F32)


def mm(a, b):
    return jnp.dot(a, b, preferred_element_type=F32)


def diagonal(ref, slot, blocks):
    row = col = 0
    for b in blocks:
        ref[slot, row : row + b.shape[0], col : col + b.shape[1]] = b
        row, col = row + b.shape[0], col + b.shape[1]


def forward_kernel(
    g, fanout, blocks, core, rhs_hbm, inv_hbm, off_hbm, keep_hbm, send_hbm,
    rhs, inv, off, acc, staged, w_inv, w_off, in_sems, out_sems,
):
    leaves = rhs.shape[0]
    _, heights, parents, block_rows, width = acc.shape
    half = heights * block_rows
    me = core[0]

    def fetches(i):
        some = pl.ds(g * i, g)
        return [
            pltpu.make_async_copy(hbm.at[some], vmem.at[some], in_sems.at[n, i])
            for n, (hbm, vmem) in enumerate(((inv_hbm, inv), (rhs_hbm, rhs), (off_hbm, off)))
        ]

    for i in range(leaves // g):
        for copy in fetches(i):
            copy.start()

    w_inv[...] = jnp.zeros_like(w_inv)
    w_off[...] = jnp.zeros_like(w_off)
    acc[...] = jnp.zeros_like(acc)

    def pair(j, slot):
        diagonal(w_inv, slot, [inv[j], inv[j + 1]])
        diagonal(w_off, slot, [off[j + h].reshape(fanout * width, width) for h in range(2)])
        x = jnp.concatenate(
            [
                jnp.concatenate(
                    [rhs[j + h, z, c] for c in (me, 1 - me) for z in range(heights)], axis=0
                )
                for h in range(2)
            ],
            axis=1,
        )
        y = mm_t(x, w_inv[slot]).astype(BF16)
        part = mm_t(y, w_off[slot])
        for h in range(2):
            for k in range(fanout):
                p = blocks[(j + h) * fanout + k]
                at = (h * fanout + k) * width
                for c in range(CORES):
                    for z in range(heights):
                        row = c * half + z * block_rows
                        acc[c, z, p] += part[row : row + block_rows, at : at + width]

    @pl.loop(0, leaves // g)
    def _(i):
        for copy in fetches(i):
            copy.wait()
        for u in range(0, g, 2):
            pair(i * g + u, (u // 2) % w_inv.shape[0])

    copies = []
    for z in range(heights):
        for c, out in ((1, send_hbm), (0, keep_hbm)):
            staged[c, z] = acc[c, z].astype(BF16)
            copies.append(pltpu.make_async_copy(staged.at[c, z], out.at[z], out_sems.at[c, z]))
            copies[-1].start()
    for copy in copies:
        copy.wait()


def forward(blocks, core, rhs, inv, off, parents):
    leaves, heights, _, block_rows, width = rhs.shape
    fanout = off.shape[1]
    half = (heights, parents, block_rows, width)
    g, slots = F_G, F_S
    smem, hbm = pl.BlockSpec(memory_space=pltpu.SMEM), pl.BlockSpec(memory_space=pltpu.HBM)
    return pl.pallas_call(
        functools.partial(forward_kernel, g, fanout),
        in_specs=[smem, smem, hbm, hbm, hbm],
        out_specs=[hbm, hbm],
        scratch_shapes=[
            pltpu.VMEM(rhs.shape, BF16),
            pltpu.VMEM(inv.shape, BF16),
            pltpu.VMEM(off.shape, BF16),
            pltpu.VMEM((CORES,) + half, F32),
            pltpu.VMEM((CORES,) + half, BF16),
            pltpu.VMEM((slots, 2 * width, 2 * width), BF16),
            pltpu.VMEM((slots, 2 * fanout * width, 2 * width), BF16),
            pltpu.SemaphoreType.DMA((3, leaves // g)),
            pltpu.SemaphoreType.DMA((CORES, heights)),
        ],
        out_shape=[jax.ShapeDtypeStruct(half, BF16)] * 2,
        compiler_params=params(32),
        name="forward",
        cost_estimate=cost(7_000_000_000, 19_000_000),
    )(blocks, core, *in_hbm(rhs, inv, off))


def fold_kernel(g, fanout, inv, off, after, out, w_inv):
    width = inv.shape[-1]

    @pl.when(pl.program_id(0) == 0)
    def _():
        w_inv[...] = jnp.zeros_like(w_inv)

    for i in range(0, g, 2):
        slot = (i // 2) % 2
        diagonal(w_inv, slot, [inv[i], inv[i + 1]])
        x = jnp.concatenate([off[i + h].reshape(fanout * width, width) for h in range(2)], axis=1)
        m = mm(x, w_inv[slot]).astype(BF16)
        for h in range(2):
            out[i + h] = m[:, h * width : (h + 1) * width]


def fold(inv, off, after):
    leaves, fanout, width, _ = off.shape
    g = 8
    return pl.pallas_call(
        functools.partial(fold_kernel, g, fanout),
        grid=(leaves // g,),
        in_specs=[
            pl.BlockSpec((g, width, width), lambda s: (s, 0, 0)),
            pl.BlockSpec((g, fanout, width, width), lambda s: (s, 0, 0, 0)),
            pl.BlockSpec(memory_space=pl.ANY),
        ],
        out_specs=pl.BlockSpec((g, fanout * width, width), lambda s: (s, 0, 0)),
        out_shape=jax.ShapeDtypeStruct((leaves, fanout * width, width), BF16),
        scratch_shapes=[pltpu.VMEM((2, 2 * width, 2 * width), BF16)],
        compiler_params=params(54),
        name="fold",
        cost_estimate=cost(4_000_000_000, 15_000_000),
    )(inv, off, after)


def leaf_kernel(g, rhs, inv, out, w_inv):
    width = inv.shape[-1]

    @pl.when(pl.program_id(0) == 0)
    def _():
        w_inv[...] = jnp.zeros_like(w_inv)

    for i in range(0, g, 2):
        slot = (i // 2) % 2
        diagonal(w_inv, slot, [inv[i], inv[i + 1]])
        x = jnp.concatenate([rhs[i], rhs[i + 1]], axis=1)
        y = mm_t(x, w_inv[slot]).astype(BF16)
        z = mm(y, w_inv[slot]).astype(BF16)
        for h in range(2):
            out[i + h] = z[:, h * width : (h + 1) * width]


def leaf(rhs, inv):
    leaves, nrhs, width = rhs.shape
    g = 8
    return pl.pallas_call(
        functools.partial(leaf_kernel, g),
        grid=(leaves // g,),
        in_specs=[
            pl.BlockSpec((g, nrhs, width), lambda s: (s, 0, 0)),
            pl.BlockSpec((g, width, width), lambda s: (s, 0, 0)),
        ],
        out_specs=pl.BlockSpec((g, nrhs, width), lambda s: (s, 0, 0)),
        out_shape=jax.ShapeDtypeStruct(rhs.shape, BF16),
        scratch_shapes=[pltpu.VMEM((2, 2 * width, 2 * width), BF16)],
        compiler_params=params(54),
        name="leaf",
        cost_estimate=cost(6_000_000_000, 20_000_000),
    )(rhs, inv)


def parent_kernel(sources, targets, got, rhs, pieces, place, after, x_out, x_every):
    own, block_rows, width = x_out.shape
    side = pieces.shape[0]
    total = got[0].astype(F32)
    for s in range(1, sources):
        total += got[s].astype(F32)
    for p in range(own):
        rest = rhs[p].astype(F32) - total[p]
        high = rest.astype(BF16)
        left = rest - high.astype(F32)
        mid = left.astype(BF16)
        low = (left - mid.astype(F32)).astype(BF16)
        w = jnp.concatenate(
            [pieces[lax.rem(place[0] - t + side, side), p] for t in range(side)], axis=0
        )
        y = (mm_t(low, w) + mm_t(mid, w)) + mm_t(high, w)
        x = mm(y.astype(BF16), w).astype(BF16)
        x_out[p] = x
        for s in range(targets):
            x_every[s, p] = x


def parent(got, rhs, pieces, place, after, targets):
    sources = got.shape[0]
    return pl.pallas_call(
        functools.partial(parent_kernel, sources, targets),
        in_specs=[pl.BlockSpec(memory_space=pltpu.VMEM)] * 3
        + [pl.BlockSpec(memory_space=pltpu.SMEM), pl.BlockSpec(memory_space=pl.ANY)],
        out_shape=[
            jax.ShapeDtypeStruct(got.shape[1:], BF16),
            jax.ShapeDtypeStruct((targets,) + got.shape[1:], BF16),
        ],
        compiler_params=params(16),
        name="parent",
        cost_estimate=cost(30_000_000, 4_500_000),
    )(got, rhs, pieces, place, after)


def backward_kernel(g, fanout, n_xs, blocks, which, base_hbm, folded_hbm, *rest):
    xs = [ref.at[n] for ref in rest[:n_xs] for n in range(ref.shape[0])]
    out_hbm, base, folded, out, w, in_sems, out_sems = rest[-7:]
    leaves, parts, block_rows, width = base.shape

    def fetches(i):
        some = pl.ds(g * i, g)
        return [
            pltpu.make_async_copy(folded_hbm.at[some], folded.at[some], in_sems.at[parts, i])
        ] + [
            pltpu.make_async_copy(base_hbm.at[some, which[n]], base.at[some, n], in_sems.at[n, i])
            for n in range(parts)
        ]

    def stores(i):
        some = pl.ds(g * i, g)
        return [
            pltpu.make_async_copy(out.at[some, n], out_hbm.at[some, which[n]], out_sems.at[n, i])
            for n in range(parts)
        ]

    for i in range(leaves // g):
        for copy in fetches(i):
            copy.start()

    w[...] = jnp.zeros_like(w)

    def pair(j, slot):
        diagonal(w, slot, [folded[j], folded[j + 1]])
        x = jnp.concatenate(
            [
                jnp.concatenate([ref[blocks[(j + h) * fanout + k]] for ref in xs], axis=0)
                for h in range(2)
                for k in range(fanout)
            ],
            axis=1,
        )
        back = mm(x, w[slot])
        for h in range(2):
            for n in range(parts):
                row = n * block_rows
                part = back[row : row + block_rows, h * width : (h + 1) * width]
                out[j + h, n] = (base[j + h, n].astype(F32) - part).astype(BF16)

    @pl.loop(0, leaves // g)
    def _(i):
        for copy in fetches(i):
            copy.wait()
        for u in range(0, g, 2):
            pair(i * g + u, (u // 2) % w.shape[0])
        for copy in stores(i):
            copy.start()

    for i in range(leaves // g):
        for copy in stores(i):
            copy.wait()


def backward(blocks, which, base, folded, xs, so_far=None):
    leaves, _, block_rows, width = base.shape
    fanout = folded.shape[1] // width
    parts = which.shape[0]
    some = (leaves, parts, block_rows, width)
    g, slots = B_G, B_S
    more = [] if so_far is None else [so_far]
    smem, hbm, vmem = (
        pl.BlockSpec(memory_space=m) for m in (pltpu.SMEM, pltpu.HBM, pltpu.VMEM)
    )
    return pl.pallas_call(
        functools.partial(backward_kernel, g, fanout, len(xs)),
        in_specs=[smem, smem, hbm, hbm] + [vmem] * len(xs) + [hbm] * len(more),
        out_specs=hbm,
        scratch_shapes=[
            pltpu.VMEM(some, BF16),
            pltpu.VMEM(folded.shape, BF16),
            pltpu.VMEM(some, BF16),
            pltpu.VMEM((slots, 2 * fanout * width, 2 * width), BF16),
            pltpu.SemaphoreType.DMA((parts + 1, leaves // g)),
            pltpu.SemaphoreType.DMA((parts, leaves // g)),
        ],
        out_shape=jax.ShapeDtypeStruct(base.shape, BF16),
        input_output_aliases={4 + len(xs): 0} if more else {},
        compiler_params=params(24),
        name="backward",
        cost_estimate=cost(5_000_000_000, 13_000_000),
    )(blocks, which, *in_hbm(base, folded), *xs, *more)


def on_device(rows, cols, leaf_rhs, leaf_inv, leaf_off, blocks, par_rhs, par_inv):
    own, block_rows, width = par_rhs.shape
    leaves, nrhs, _ = leaf_rhs.shape
    parents = own * cols
    side = rows // CORES
    deep = cols // side
    both = ("row", "col")

    def device(u, c, v, y):
        z, x = (u % side, v) if c == 0 else (v, u % side)
        return (z * CORES + c) * cols + x * deep + y

    every = [
        (u, c, v, y)
        for u in range(side)
        for c in range(CORES)
        for v in range(side)
        for y in range(deep)
    ]
    turn = [(device(u, 0, v, y) + (cols if c else 0), device(u, c, v, y)) for u, c, v, y in every]
    swap = [(r, r ^ 1) for r in range(rows)]
    row, col = lax.axis_index("row"), lax.axis_index("col")
    core = (row % CORES).astype(jnp.int32)
    z, x = (row // CORES).astype(jnp.int32), (col // deep).astype(jnp.int32)
    u, other_u = jnp.where(core == 0, z, x), jnp.where(core == 0, x, z)

    def along(a, step):
        return lax.ppermute(
            a, both, [(device(u, c, v, y), device(u + step, c, v, y)) for u, c, v, y in every]
        )

    def spread(a, first, stride):
        groups = [
            [device(u, c, v, y) for u in range(f, side, stride) for v in range(side) for y in range(deep)]
            for c in range(CORES)
            for f in first
        ]
        return lax.all_to_all(a, both, 0, 0, axis_index_groups=groups, tiled=True)

    by_core = (leaves, side, CORES, block_rows, width)

    flat = blocks.reshape(-1)
    across = lax.ppermute(par_inv, "row", swap)
    keep, send = forward(flat, core.reshape(1), leaf_rhs.reshape(by_core), leaf_inv, leaf_off, parents)
    across, send = lax.optimization_barrier((across, send))
    low, high = jnp.where(core == 0, par_inv, across), jnp.where(core == 0, across, par_inv)
    given = lax.ppermute(jnp.concatenate([par_rhs, low, high], axis=1), both, turn)
    received = lax.ppermute(send, "row", swap)
    chip = (keep.astype(F32) + received.astype(F32)).astype(BF16)
    chip, given = lax.optimization_barrier((chip, given))
    pair = given[:, block_rows:]
    shifts = [pair] + [along(pair, step) for step in range(1, side)]
    got = spread(chip.reshape(side * cols, own, block_rows, width), (0,), 1)
    base = leaf(leaf_rhs, leaf_inv)
    pieces = jnp.stack(shifts)
    par_x, targets = parent(
        got, given[:, :block_rows], pieces, u.reshape(1), base[0, :16], side // 2 * cols
    )
    near = spread(targets, (0, 1), 2).reshape(side // 2, parents, block_rows, width)
    folded = fold(leaf_inv, leaf_off, par_x)
    near, base, folded, x_out = lax.optimization_barrier(
        (near, base, folded, lax.ppermute(par_x, both, turn))
    )
    base = base.reshape(leaves, rows, block_rows, width)

    mine = jnp.where(u < 2, near[:1], near[1:])
    near_other = lax.ppermute(near, "row", swap)
    far = [along(mine, -1), along(mine, 1)]

    def places(us, other_us):
        return jnp.stack(
            [(a % side) * CORES + core for a in us] + [(a % side) * CORES + 1 - core for a in other_us]
        ).astype(jnp.int32)

    first = places((u % 2, u % 2 + 2), (other_u % 2, other_u % 2 + 2))
    second = places((u + 1, u + side - 1), (other_u + 1, other_u + side - 1))
    half = backward(flat, first, base, folded, [near, near_other])
    far, half = lax.optimization_barrier((far, half))
    far_other = [lax.ppermute(a, "row", swap) for a in far]
    leaf_x = backward(flat, second, base, folded, far + far_other, half)
    return (leaf_x.reshape(leaf_rhs.shape), x_out)


def solution(mesh):
    rows, cols = mesh.shape["row"], mesh.shape["col"]
    return jax.shard_map(
        functools.partial(on_device, rows, cols),
        mesh=mesh,
        in_specs=(
            P(("row", "col"), None, None),
            P(("row", "col"), None, None),
            P(("row", "col"), None, None, None),
            P(("row", "col"), None),
            P("col", "row", None),
            P("col", "row", None),
        ),
        out_specs=(P(("row", "col"), None, None), P("col", "row", None)),
        check_vma=False,
    )
```

```python
import functools

import jax
import jax.numpy as jnp
from jax import lax
from jax.experimental import pallas as pl
from jax.experimental.pallas import tpu as pltpu
from jax.sharding import PartitionSpec as P

F32, BF16 = jnp.float32, jnp.bfloat16
F_G, F_S, B_G, B_S = 12, 2, 12, 2
CORES = 2


def params(mib):
    return pltpu.CompilerParams(vmem_limit_bytes=mib * 1024 * 1024)


def in_hbm(*arrays):
    return [pltpu.with_memory_space_constraint(a, pltpu.HBM) for a in arrays]


def cost(flops, moved):
    return pl.CostEstimate(flops=flops, bytes_accessed=moved, transcendentals=0)


def mm_t(a, b):
    return lax.dot_general(a, b, (((1,), (1,)), ((), ())), preferred_element_type=F32)


def mm(a, b):
    return jnp.dot(a, b, preferred_element_type=F32)


def diagonal(ref, slot, blocks):
    row = col = 0
    for b in blocks:
        ref[slot, row : row + b.shape[0], col : col + b.shape[1]] = b
        row, col = row + b.shape[0], col + b.shape[1]


def forward_kernel(
    g, fanout, blocks, which, rhs_hbm, inv_hbm, off_hbm, *rest
):
    outs, (rhs, inv, off, acc, staged, w_inv, w_off, in_sems, out_sems) = rest[:-9], rest[-9:]
    leaves = rhs.shape[0]
    parts, parents, block_rows, width = acc.shape

    def fetches(i):
        some = pl.ds(g * i, g)
        return [
            pltpu.make_async_copy(hbm.at[some], vmem.at[some], in_sems.at[n, i])
            for n, (hbm, vmem) in enumerate(((inv_hbm, inv), (rhs_hbm, rhs), (off_hbm, off)))
        ]

    for i in range(leaves // g):
        for copy in fetches(i):
            copy.start()

    w_inv[...] = jnp.zeros_like(w_inv)
    w_off[...] = jnp.zeros_like(w_off)
    acc[...] = jnp.zeros_like(acc)

    def pair(j, slot):
        diagonal(w_inv, slot, [inv[j], inv[j + 1]])
        diagonal(w_off, slot, [off[j + h].reshape(fanout * width, width) for h in range(2)])
        x = jnp.concatenate(
            [
                jnp.concatenate([rhs[j + h, which[n]] for n in range(parts)], axis=0)
                for h in range(2)
            ],
            axis=1,
        )
        y = mm_t(x, w_inv[slot]).astype(BF16)
        part = mm_t(y, w_off[slot])
        for h in range(2):
            for k in range(fanout):
                p = blocks[(j + h) * fanout + k]
                at = (h * fanout + k) * width
                for n in range(parts):
                    row = n * block_rows
                    acc[n, p] += part[row : row + block_rows, at : at + width]

    @pl.loop(0, leaves // g)
    def _(i):
        for copy in fetches(i):
            copy.wait()
        for u in range(0, g, 2):
            pair(i * g + u, (u // 2) % w_inv.shape[0])

    copies = []
    each = outs[0].shape[0]
    for n in range(parts):
        staged[n] = acc[n].astype(BF16)
        copies.append(
            pltpu.make_async_copy(staged.at[n], outs[n // each].at[n % each], out_sems.at[n])
        )
        copies[-1].start()
    for copy in copies:
        copy.wait()


def forward(blocks, which, rhs, inv, off, parents, each):
    leaves, parts, block_rows, width = rhs.shape
    fanout = off.shape[1]
    one = (parents, block_rows, width)
    g, slots = F_G, F_S
    smem, hbm = pl.BlockSpec(memory_space=pltpu.SMEM), pl.BlockSpec(memory_space=pltpu.HBM)
    return pl.pallas_call(
        functools.partial(forward_kernel, g, fanout),
        in_specs=[smem, smem, hbm, hbm, hbm],
        out_specs=[hbm] * (parts // each),
        scratch_shapes=[
            pltpu.VMEM(rhs.shape, BF16),
            pltpu.VMEM(inv.shape, BF16),
            pltpu.VMEM(off.shape, BF16),
            pltpu.VMEM((parts,) + one, F32),
            pltpu.VMEM((parts,) + one, BF16),
            pltpu.VMEM((slots, 2 * width, 2 * width), BF16),
            pltpu.VMEM((slots, 2 * fanout * width, 2 * width), BF16),
            pltpu.SemaphoreType.DMA((3, leaves // g)),
            pltpu.SemaphoreType.DMA((parts,)),
        ],
        out_shape=[jax.ShapeDtypeStruct((each,) + one, BF16)] * (parts // each),
        compiler_params=params(32),
        name="forward",
        cost_estimate=cost(7_000_000_000, 19_000_000),
    )(blocks, which, *in_hbm(rhs, inv, off))


def fold_kernel(g, fanout, inv, off, out, w_inv):
    width = inv.shape[-1]

    @pl.when(pl.program_id(0) == 0)
    def _():
        w_inv[...] = jnp.zeros_like(w_inv)

    for i in range(0, g, 2):
        slot = (i // 2) % 2
        diagonal(w_inv, slot, [inv[i], inv[i + 1]])
        x = jnp.concatenate([off[i + h].reshape(fanout * width, width) for h in range(2)], axis=1)
        m = mm(x, w_inv[slot]).astype(BF16)
        for h in range(2):
            out[i + h] = m[:, h * width : (h + 1) * width]


def fold(inv, off):
    leaves, fanout, width, _ = off.shape
    g = 8
    return pl.pallas_call(
        functools.partial(fold_kernel, g, fanout),
        grid=(leaves // g,),
        in_specs=[
            pl.BlockSpec((g, width, width), lambda s: (s, 0, 0)),
            pl.BlockSpec((g, fanout, width, width), lambda s: (s, 0, 0, 0)),
        ],
        out_specs=pl.BlockSpec((g, fanout * width, width), lambda s: (s, 0, 0)),
        out_shape=jax.ShapeDtypeStruct((leaves, fanout * width, width), BF16),
        scratch_shapes=[pltpu.VMEM((2, 2 * width, 2 * width), BF16)],
        compiler_params=params(54),
        name="fold",
        cost_estimate=cost(4_000_000_000, 15_000_000),
    )(inv, off)


def leaf_kernel(g, rhs, inv, after, out, w_inv):
    width = inv.shape[-1]

    @pl.when(pl.program_id(0) == 0)
    def _():
        w_inv[...] = jnp.zeros_like(w_inv)

    for i in range(0, g, 2):
        slot = (i // 2) % 2
        diagonal(w_inv, slot, [inv[i], inv[i + 1]])
        x = jnp.concatenate([rhs[i], rhs[i + 1]], axis=1)
        y = mm_t(x, w_inv[slot]).astype(BF16)
        z = mm(y, w_inv[slot]).astype(BF16)
        for h in range(2):
            out[i + h] = z[:, h * width : (h + 1) * width]


def leaf(rhs, inv, after):
    leaves, nrhs, width = rhs.shape
    g = 8
    return pl.pallas_call(
        functools.partial(leaf_kernel, g),
        grid=(leaves // g,),
        in_specs=[
            pl.BlockSpec((g, nrhs, width), lambda s: (s, 0, 0)),
            pl.BlockSpec((g, width, width), lambda s: (s, 0, 0)),
            pl.BlockSpec(memory_space=pl.ANY),
        ],
        out_specs=pl.BlockSpec((g, nrhs, width), lambda s: (s, 0, 0)),
        out_shape=jax.ShapeDtypeStruct(rhs.shape, BF16),
        scratch_shapes=[pltpu.VMEM((2, 2 * width, 2 * width), BF16)],
        compiler_params=params(54),
        name="leaf",
        cost_estimate=cost(6_000_000_000, 20_000_000),
    )(rhs, inv, after)


def parent_kernel(sources, targets, side, got, given, place, after, x_out, x_every):
    own, block_rows, width = x_out.shape
    part = width // side
    total = got[0].astype(F32)
    for s in range(1, sources):
        total += got[s].astype(F32)
    for p in range(own):
        rest = given[p, :block_rows].astype(F32) - total[p]
        high = rest.astype(BF16)
        left = rest - high.astype(F32)
        mid = left.astype(BF16)
        low = (left - mid.astype(F32)).astype(BF16)
        w = jnp.concatenate(
            [
                given[
                    p,
                    pl.ds(
                        pl.multiple_of(block_rows + lax.rem(place[0] - t + side, side) * part, 16), part
                    ),
                ]
                for t in range(side)
            ],
            axis=0,
        )
        y = (mm_t(low, w) + mm_t(mid, w)) + mm_t(high, w)
        x = mm(y.astype(BF16), w).astype(BF16)
        x_out[p] = x
        for s in range(targets):
            x_every[s, p] = x


def parent(got, given, side, place, after, targets):
    sources = got.shape[0]
    return pl.pallas_call(
        functools.partial(parent_kernel, sources, targets, side),
        in_specs=[pl.BlockSpec(memory_space=pltpu.VMEM)] * 2
        + [pl.BlockSpec(memory_space=pltpu.SMEM), pl.BlockSpec(memory_space=pl.ANY)],
        out_shape=[
            jax.ShapeDtypeStruct(got.shape[1:], BF16),
            jax.ShapeDtypeStruct((targets,) + got.shape[1:], BF16),
        ],
        compiler_params=params(16),
        name="parent",
        cost_estimate=cost(30_000_000, 4_500_000),
    )(got, given, place, after)


def backward_kernel(g, fanout, n_xs, blocks, which, base_hbm, folded_hbm, *rest):
    xs = [ref.at[n] for ref in rest[:n_xs] for n in range(ref.shape[0])]
    out_hbm, base, folded, out, w, in_sems, out_sems = rest[-7:]
    leaves, parts, block_rows, width = base.shape

    def fetches(i):
        some = pl.ds(g * i, g)
        return [
            pltpu.make_async_copy(folded_hbm.at[some], folded.at[some], in_sems.at[parts, i])
        ] + [
            pltpu.make_async_copy(base_hbm.at[some, which[n]], base.at[some, n], in_sems.at[n, i])
            for n in range(parts)
        ]

    def stores(i):
        some = pl.ds(g * i, g)
        return [
            pltpu.make_async_copy(out.at[some, n], out_hbm.at[some, which[n]], out_sems.at[n, i])
            for n in range(parts)
        ]

    for i in range(leaves // g):
        for copy in fetches(i):
            copy.start()

    w[...] = jnp.zeros_like(w)

    def pair(j, slot):
        diagonal(w, slot, [folded[j], folded[j + 1]])
        x = jnp.concatenate(
            [
                jnp.concatenate([ref[blocks[(j + h) * fanout + k]] for ref in xs], axis=0)
                for h in range(2)
                for k in range(fanout)
            ],
            axis=1,
        )
        back = mm(x, w[slot])
        for h in range(2):
            for n in range(parts):
                row = n * block_rows
                part = back[row : row + block_rows, h * width : (h + 1) * width]
                out[j + h, n] = (base[j + h, n].astype(F32) - part).astype(BF16)

    @pl.loop(0, leaves // g)
    def _(i):
        for copy in fetches(i):
            copy.wait()
        for u in range(0, g, 2):
            pair(i * g + u, (u // 2) % w.shape[0])
        for copy in stores(i):
            copy.start()

    for i in range(leaves // g):
        for copy in stores(i):
            copy.wait()


def backward(blocks, which, base, folded, xs, so_far=None):
    leaves, _, block_rows, width = base.shape
    fanout = folded.shape[1] // width
    parts = which.shape[0]
    some = (leaves, parts, block_rows, width)
    g, slots = B_G, B_S
    more = [] if so_far is None else [so_far]
    smem, hbm, vmem = (
        pl.BlockSpec(memory_space=m) for m in (pltpu.SMEM, pltpu.HBM, pltpu.VMEM)
    )
    return pl.pallas_call(
        functools.partial(backward_kernel, g, fanout, len(xs)),
        in_specs=[smem, smem, hbm, hbm] + [vmem] * len(xs) + [hbm] * len(more),
        out_specs=hbm,
        scratch_shapes=[
            pltpu.VMEM(some, BF16),
            pltpu.VMEM(folded.shape, BF16),
            pltpu.VMEM(some, BF16),
            pltpu.VMEM((slots, 2 * fanout * width, 2 * width), BF16),
            pltpu.SemaphoreType.DMA((parts + 1, leaves // g)),
            pltpu.SemaphoreType.DMA((parts, leaves // g)),
        ],
        out_shape=jax.ShapeDtypeStruct(base.shape, BF16),
        input_output_aliases={4 + len(xs): 0} if more else {},
        compiler_params=params(24),
        name="backward",
        cost_estimate=cost(5_000_000_000, 13_000_000),
    )(blocks, which, *in_hbm(base, folded), *xs, *more)


def on_device(rows, cols, leaf_rhs, leaf_inv, leaf_off, blocks, par_rhs, par_inv):
    own, block_rows, width = par_rhs.shape
    leaves, nrhs, _ = leaf_rhs.shape
    parents = own * cols
    side = rows // CORES
    deep = cols // side
    both = ("row", "col")

    def device(u, c, v, y):
        z, x = (u % side, v) if c == 0 else (v, u % side)
        return (z * CORES + c) * cols + x * deep + y

    every = [
        (u, c, v, y)
        for u in range(side)
        for c in range(CORES)
        for v in range(side)
        for y in range(deep)
    ]
    turn = [(device(u, 0, v, y) + (cols if c else 0), device(u, c, v, y)) for u, c, v, y in every]
    swap = [(r, r ^ 1) for r in range(rows)]
    row, col = lax.axis_index("row"), lax.axis_index("col")
    core = (row % CORES).astype(jnp.int32)
    z, x = (row // CORES).astype(jnp.int32), (col // deep).astype(jnp.int32)
    u, other_u = jnp.where(core == 0, z, x), jnp.where(core == 0, x, z)

    def along(a, step):
        return lax.ppermute(
            a, both, [(device(u, c, v, y), device(u + step, c, v, y)) for u, c, v, y in every]
        )

    def spread(a, first, stride):
        groups = [
            [device(u, c, v, y) for u in range(f, side, stride) for v in range(side) for y in range(deep)]
            for c in range(CORES)
            for f in first
        ]
        return lax.all_to_all(a, both, 0, 0, axis_index_groups=groups, tiled=True)

    by_block = (leaves, rows, block_rows, width)

    def places(us, other_us):
        return jnp.stack(
            [(a % side) * CORES + core for a in us] + [(a % side) * CORES + 1 - core for a in other_us]
        ).astype(jnp.int32)

    near_places = places((u % 2, u % 2 + 2), (other_u % 2, other_u % 2 + 2))
    far_places = places((u + 1, u + side - 1), (other_u + 1, other_u + side - 1))

    flat = blocks.reshape(-1)
    across = lax.ppermute(par_inv, "row", swap)
    keep_far, send_far, keep_near, send_near = forward(
        flat,
        jnp.concatenate([far_places, near_places]),
        leaf_rhs.reshape(by_block),
        leaf_inv,
        leaf_off,
        parents,
        2,
    )
    across, send_far = lax.optimization_barrier((across, send_far))
    low, high = jnp.where(core == 0, par_inv, across), jnp.where(core == 0, across, par_inv)
    pair = jnp.concatenate([low, high], axis=1)
    shifts = [pair] + [
        lax.ppermute(pair, "row", [(r, (r + CORES * s) % rows) for r in range(rows)])
        for s in range(1, side)
    ]
    far = [
        (keep_far[n : n + 1].astype(F32) + lax.ppermute(send_far, "row", swap)[n : n + 1].astype(F32)).astype(BF16)
        for n in range(2)
    ]
    received = lax.ppermute(send_near, "row", swap)
    neighbours = along(far[0], 1).astype(F32) + along(far[1], -1).astype(F32)
    here = jnp.arange(2, dtype=jnp.int32).reshape(2, 1, 1, 1) == u // 2
    chip = keep_near.astype(F32) + received.astype(F32) + jnp.where(here, neighbours, 0.0)
    chip = chip.astype(BF16)
    chip, shifts = lax.optimization_barrier((chip, shifts))
    got = spread(chip.reshape(side // 2 * cols, own, block_rows, width), (0, 1), 2)
    folded = fold(leaf_inv, leaf_off)
    given = lax.ppermute(jnp.concatenate([par_rhs] + shifts, axis=1), both, turn)
    par_x, targets = parent(got, given, side, u.reshape(1), folded[0, :16], side // 2 * cols)
    near = spread(targets, (0, 1), 2).reshape(side // 2, parents, block_rows, width)
    base = leaf(leaf_rhs, leaf_inv, par_x)
    near, base, folded, x_out = lax.optimization_barrier(
        (near, base, folded, lax.ppermute(par_x, both, turn))
    )
    base = base.reshape(by_block)

    mine = jnp.where(u < 2, near[:1], near[1:])
    near_other = lax.ppermute(near, "row", swap)
    far = [along(mine, -1), along(mine, 1)]

    half = backward(flat, near_places, base, folded, [near, near_other])
    far, half = lax.optimization_barrier((far, half))
    far_other = [lax.ppermute(a, "row", swap) for a in far]
    leaf_x = backward(flat, far_places, base, folded, far + far_other, half)
    return (leaf_x.reshape(leaf_rhs.shape), x_out)


def solution(mesh):
    rows, cols = mesh.shape["row"], mesh.shape["col"]
    return jax.shard_map(
        functools.partial(on_device, rows, cols),
        mesh=mesh,
        in_specs=(
            P(("row", "col"), None, None),
            P(("row", "col"), None, None),
            P(("row", "col"), None, None, None),
            P(("row", "col"), None),
            P("col", "row", None),
            P("col", "row", None),
        ),
        out_specs=(P(("row", "col"), None, None), P("col", "row", None)),
        check_vma=False,
    )
```

```python
import functools

import jax
import jax.numpy as jnp
from jax import lax
from jax.experimental import pallas as pl
from jax.experimental.pallas import tpu as pltpu
from jax.sharding import PartitionSpec as P

F32, BF16 = jnp.float32, jnp.bfloat16
F_G, F_S, B_G, B_S = 12, 2, 12, 2
CORES = 2


def params(mib):
    return pltpu.CompilerParams(vmem_limit_bytes=mib * 1024 * 1024)


def in_hbm(*arrays):
    return [pltpu.with_memory_space_constraint(a, pltpu.HBM) for a in arrays]


def cost(flops, moved):
    return pl.CostEstimate(flops=flops, bytes_accessed=moved, transcendentals=0)


def mm_t(a, b):
    return lax.dot_general(a, b, (((1,), (1,)), ((), ())), preferred_element_type=F32)


def mm(a, b):
    return jnp.dot(a, b, preferred_element_type=F32)


def diagonal(ref, slot, blocks):
    row = col = 0
    for b in blocks:
        ref[slot, row : row + b.shape[0], col : col + b.shape[1]] = b
        row, col = row + b.shape[0], col + b.shape[1]


def forward_kernel(
    g, fanout, blocks, which, rhs_hbm, inv_hbm, off_hbm, *rest
):
    outs, (rhs, inv, off, acc, staged, w_inv, w_off, in_sems, out_sems) = rest[:-9], rest[-9:]
    leaves = rhs.shape[0]
    parts, parents, block_rows, width = acc.shape

    def fetches(i):
        some = pl.ds(g * i, g)
        return [
            pltpu.make_async_copy(hbm.at[some], vmem.at[some], in_sems.at[n, i])
            for n, (hbm, vmem) in enumerate(((inv_hbm, inv), (rhs_hbm, rhs), (off_hbm, off)))
        ]

    for i in range(leaves // g):
        for copy in fetches(i):
            copy.start()

    w_inv[...] = jnp.zeros_like(w_inv)
    w_off[...] = jnp.zeros_like(w_off)
    acc[...] = jnp.zeros_like(acc)

    def pair(j, slot):
        diagonal(w_inv, slot, [inv[j], inv[j + 1]])
        diagonal(w_off, slot, [off[j + h].reshape(fanout * width, width) for h in range(2)])
        x = jnp.concatenate(
            [
                jnp.concatenate([rhs[j + h, which[n]] for n in range(parts)], axis=0)
                for h in range(2)
            ],
            axis=1,
        )
        y = mm_t(x, w_inv[slot]).astype(BF16)
        part = mm_t(y, w_off[slot])
        for h in range(2):
            for k in range(fanout):
                p = blocks[(j + h) * fanout + k]
                at = (h * fanout + k) * width
                for n in range(parts):
                    row = n * block_rows
                    acc[n, p] += part[row : row + block_rows, at : at + width]

    @pl.loop(0, leaves // g)
    def _(i):
        for copy in fetches(i):
            copy.wait()
        for u in range(0, g, 2):
            pair(i * g + u, (u // 2) % w_inv.shape[0])

    copies = []
    each = outs[0].shape[0]
    for n in range(parts):
        staged[n] = acc[n].astype(BF16)
        copies.append(
            pltpu.make_async_copy(staged.at[n], outs[n // each].at[n % each], out_sems.at[n])
        )
        copies[-1].start()
    for copy in copies:
        copy.wait()


def forward(blocks, which, rhs, inv, off, parents, each):
    leaves, parts, block_rows, width = rhs.shape
    fanout = off.shape[1]
    one = (parents, block_rows, width)
    g, slots = F_G, F_S
    smem, hbm = pl.BlockSpec(memory_space=pltpu.SMEM), pl.BlockSpec(memory_space=pltpu.HBM)
    return pl.pallas_call(
        functools.partial(forward_kernel, g, fanout),
        in_specs=[smem, smem, hbm, hbm, hbm],
        out_specs=[hbm] * (parts // each),
        scratch_shapes=[
            pltpu.VMEM(rhs.shape, BF16),
            pltpu.VMEM(inv.shape, BF16),
            pltpu.VMEM(off.shape, BF16),
            pltpu.VMEM((parts,) + one, F32),
            pltpu.VMEM((parts,) + one, BF16),
            pltpu.VMEM((slots, 2 * width, 2 * width), BF16),
            pltpu.VMEM((slots, 2 * fanout * width, 2 * width), BF16),
            pltpu.SemaphoreType.DMA((3, leaves // g)),
            pltpu.SemaphoreType.DMA((parts,)),
        ],
        out_shape=[jax.ShapeDtypeStruct((each,) + one, BF16)] * (parts // each),
        compiler_params=params(32),
        name="forward",
        cost_estimate=cost(7_000_000_000, 19_000_000),
    )(blocks, which, *in_hbm(rhs, inv, off))


def fold_kernel(g, fanout, inv, off, after, out, w_inv):
    width = inv.shape[-1]

    @pl.when(pl.program_id(0) == 0)
    def _():
        w_inv[...] = jnp.zeros_like(w_inv)

    for i in range(0, g, 2):
        slot = (i // 2) % 2
        diagonal(w_inv, slot, [inv[i], inv[i + 1]])
        x = jnp.concatenate([off[i + h].reshape(fanout * width, width) for h in range(2)], axis=1)
        m = mm(x, w_inv[slot]).astype(BF16)
        for h in range(2):
            out[i + h] = m[:, h * width : (h + 1) * width]


def fold(inv, off, after):
    leaves, fanout, width, _ = off.shape
    g = 8
    return pl.pallas_call(
        functools.partial(fold_kernel, g, fanout),
        grid=(leaves // g,),
        in_specs=[
            pl.BlockSpec((g, width, width), lambda s: (s, 0, 0)),
            pl.BlockSpec((g, fanout, width, width), lambda s: (s, 0, 0, 0)),
            pl.BlockSpec(memory_space=pl.ANY),
        ],
        out_specs=pl.BlockSpec((g, fanout * width, width), lambda s: (s, 0, 0)),
        out_shape=jax.ShapeDtypeStruct((leaves, fanout * width, width), BF16),
        scratch_shapes=[pltpu.VMEM((2, 2 * width, 2 * width), BF16)],
        compiler_params=params(54),
        name="fold",
        cost_estimate=cost(4_000_000_000, 15_000_000),
    )(inv, off, after)


def leaf_kernel(g, rhs, inv, out, w_inv):
    width = inv.shape[-1]

    @pl.when(pl.program_id(0) == 0)
    def _():
        w_inv[...] = jnp.zeros_like(w_inv)

    for i in range(0, g, 2):
        slot = (i // 2) % 2
        diagonal(w_inv, slot, [inv[i], inv[i + 1]])
        x = jnp.concatenate([rhs[i], rhs[i + 1]], axis=1)
        y = mm_t(x, w_inv[slot]).astype(BF16)
        z = mm(y, w_inv[slot]).astype(BF16)
        for h in range(2):
            out[i + h] = z[:, h * width : (h + 1) * width]


def leaf(rhs, inv):
    leaves, nrhs, width = rhs.shape
    g = 8
    return pl.pallas_call(
        functools.partial(leaf_kernel, g),
        grid=(leaves // g,),
        in_specs=[
            pl.BlockSpec((g, nrhs, width), lambda s: (s, 0, 0)),
            pl.BlockSpec((g, width, width), lambda s: (s, 0, 0)),
        ],
        out_specs=pl.BlockSpec((g, nrhs, width), lambda s: (s, 0, 0)),
        out_shape=jax.ShapeDtypeStruct(rhs.shape, BF16),
        scratch_shapes=[pltpu.VMEM((2, 2 * width, 2 * width), BF16)],
        compiler_params=params(54),
        name="leaf",
        cost_estimate=cost(6_000_000_000, 20_000_000),
    )(rhs, inv)


def parent_kernel(sources, targets, side, got, given, place, after, x_out, x_every):
    own, block_rows, width = x_out.shape
    part = width // side
    total = got[0].astype(F32)
    for s in range(1, sources):
        total += got[s].astype(F32)
    for p in range(own):
        rest = given[p, :block_rows].astype(F32) - total[p]
        high = rest.astype(BF16)
        left = rest - high.astype(F32)
        mid = left.astype(BF16)
        low = (left - mid.astype(F32)).astype(BF16)
        w = jnp.concatenate(
            [
                given[
                    p,
                    pl.ds(
                        pl.multiple_of(block_rows + lax.rem(place[0] - t + side, side) * part, 16), part
                    ),
                ]
                for t in range(side)
            ],
            axis=0,
        )
        y = (mm_t(low, w) + mm_t(mid, w)) + mm_t(high, w)
        x = mm(y.astype(BF16), w).astype(BF16)
        x_out[p] = x
        for s in range(targets):
            x_every[s, p] = x


def parent(got, given, side, place, after, targets):
    sources = got.shape[0]
    return pl.pallas_call(
        functools.partial(parent_kernel, sources, targets, side),
        in_specs=[pl.BlockSpec(memory_space=pltpu.VMEM)] * 2
        + [pl.BlockSpec(memory_space=pltpu.SMEM), pl.BlockSpec(memory_space=pl.ANY)],
        out_shape=[
            jax.ShapeDtypeStruct(got.shape[1:], BF16),
            jax.ShapeDtypeStruct((targets,) + got.shape[1:], BF16),
        ],
        compiler_params=params(16),
        name="parent",
        cost_estimate=cost(30_000_000, 4_500_000),
    )(got, given, place, after)


def backward_kernel(g, fanout, n_xs, blocks, which, base_hbm, folded_hbm, *rest):
    xs = [ref.at[n] for ref in rest[:n_xs] for n in range(ref.shape[0])]
    out_hbm, base, folded, out, w, in_sems, out_sems = rest[-7:]
    leaves, parts, block_rows, width = base.shape

    def fetches(i):
        some = pl.ds(g * i, g)
        return [
            pltpu.make_async_copy(folded_hbm.at[some], folded.at[some], in_sems.at[parts, i])
        ] + [
            pltpu.make_async_copy(base_hbm.at[some, which[n]], base.at[some, n], in_sems.at[n, i])
            for n in range(parts)
        ]

    def stores(i):
        some = pl.ds(g * i, g)
        return [
            pltpu.make_async_copy(out.at[some, n], out_hbm.at[some, which[n]], out_sems.at[n, i])
            for n in range(parts)
        ]

    for i in range(leaves // g):
        for copy in fetches(i):
            copy.start()

    w[...] = jnp.zeros_like(w)

    def pair(j, slot):
        diagonal(w, slot, [folded[j], folded[j + 1]])
        x = jnp.concatenate(
            [
                jnp.concatenate([ref[blocks[(j + h) * fanout + k]] for ref in xs], axis=0)
                for h in range(2)
                for k in range(fanout)
            ],
            axis=1,
        )
        back = mm(x, w[slot])
        for h in range(2):
            for n in range(parts):
                row = n * block_rows
                part = back[row : row + block_rows, h * width : (h + 1) * width]
                out[j + h, n] = (base[j + h, n].astype(F32) - part).astype(BF16)

    @pl.loop(0, leaves // g)
    def _(i):
        for copy in fetches(i):
            copy.wait()
        for u in range(0, g, 2):
            pair(i * g + u, (u // 2) % w.shape[0])
        for copy in stores(i):
            copy.start()

    for i in range(leaves // g):
        for copy in stores(i):
            copy.wait()


def backward(blocks, which, base, folded, xs, so_far=None):
    leaves, _, block_rows, width = base.shape
    fanout = folded.shape[1] // width
    parts = which.shape[0]
    some = (leaves, parts, block_rows, width)
    g, slots = B_G, B_S
    more = [] if so_far is None else [so_far]
    smem, hbm, vmem = (
        pl.BlockSpec(memory_space=m) for m in (pltpu.SMEM, pltpu.HBM, pltpu.VMEM)
    )
    return pl.pallas_call(
        functools.partial(backward_kernel, g, fanout, len(xs)),
        in_specs=[smem, smem, hbm, hbm] + [vmem] * len(xs) + [hbm] * len(more),
        out_specs=hbm,
        scratch_shapes=[
            pltpu.VMEM(some, BF16),
            pltpu.VMEM(folded.shape, BF16),
            pltpu.VMEM(some, BF16),
            pltpu.VMEM((slots, 2 * fanout * width, 2 * width), BF16),
            pltpu.SemaphoreType.DMA((parts + 1, leaves // g)),
            pltpu.SemaphoreType.DMA((parts, leaves // g)),
        ],
        out_shape=jax.ShapeDtypeStruct(base.shape, BF16),
        input_output_aliases={4 + len(xs): 0} if more else {},
        compiler_params=params(24),
        name="backward",
        cost_estimate=cost(5_000_000_000, 13_000_000),
    )(blocks, which, *in_hbm(base, folded), *xs, *more)


def on_device(rows, cols, leaf_rhs, leaf_inv, leaf_off, blocks, par_rhs, par_inv):
    own, block_rows, width = par_rhs.shape
    leaves, nrhs, _ = leaf_rhs.shape
    parents = own * cols
    side = rows // CORES
    deep = cols // side
    both = ("row", "col")

    def device(u, c, v, y):
        z, x = (u % side, v) if c == 0 else (v, u % side)
        return (z * CORES + c) * cols + x * deep + y

    every = [
        (u, c, v, y)
        for u in range(side)
        for c in range(CORES)
        for v in range(side)
        for y in range(deep)
    ]
    turn = [(device(u, 0, v, y) + (cols if c else 0), device(u, c, v, y)) for u, c, v, y in every]
    swap = [(r, r ^ 1) for r in range(rows)]
    row, col = lax.axis_index("row"), lax.axis_index("col")
    core = (row % CORES).astype(jnp.int32)
    z, x = (row // CORES).astype(jnp.int32), (col // deep).astype(jnp.int32)
    u, other_u = jnp.where(core == 0, z, x), jnp.where(core == 0, x, z)

    def along(a, step):
        return lax.ppermute(
            a, both, [(device(u, c, v, y), device(u + step, c, v, y)) for u, c, v, y in every]
        )

    def spread(a, first, stride):
        groups = [
            [device(u, c, v, y) for u in range(f, side, stride) for v in range(side) for y in range(deep)]
            for c in range(CORES)
            for f in first
        ]
        return lax.all_to_all(a, both, 0, 0, axis_index_groups=groups, tiled=True)

    by_block = (leaves, rows, block_rows, width)

    def places(us, other_us):
        return jnp.stack(
            [(a % side) * CORES + core for a in us] + [(a % side) * CORES + 1 - core for a in other_us]
        ).astype(jnp.int32)

    near_places = places((u % 2, u % 2 + 2), (other_u % 2, other_u % 2 + 2))
    far_places = places((u + 1, u + side - 1), (other_u + 1, other_u + side - 1))

    flat = blocks.reshape(-1)
    across = lax.ppermute(par_inv, "row", swap)
    keep_far, send_far, keep_near, send_near = forward(
        flat,
        jnp.concatenate([far_places, near_places]),
        leaf_rhs.reshape(by_block),
        leaf_inv,
        leaf_off,
        parents,
        2,
    )
    across, send_far = lax.optimization_barrier((across, send_far))
    low, high = jnp.where(core == 0, par_inv, across), jnp.where(core == 0, across, par_inv)
    pair = jnp.concatenate([low, high], axis=1)
    shifts = [pair] + [
        lax.ppermute(pair, "row", [(r, (r + CORES * s) % rows) for r in range(rows)])
        for s in range(1, side)
    ]
    far = [
        (keep_far[n : n + 1].astype(F32) + lax.ppermute(send_far, "row", swap)[n : n + 1].astype(F32)).astype(BF16)
        for n in range(2)
    ]
    received = lax.ppermute(send_near, "row", swap)
    neighbours = along(far[0], 1).astype(F32) + along(far[1], -1).astype(F32)
    chip = jnp.concatenate(
        [
            (
                keep_near[n : n + 1].astype(F32)
                + received[n : n + 1].astype(F32)
                + jnp.where(u // 2 == n, neighbours, 0.0)
            ).astype(BF16)
            for n in range(2)
        ]
    )
    chip, shifts = lax.optimization_barrier((chip, shifts))
    got = spread(chip.reshape(side // 2 * cols, own, block_rows, width), (0, 1), 2)
    base = leaf(leaf_rhs, leaf_inv)
    given = lax.ppermute(jnp.concatenate([par_rhs] + shifts, axis=1), both, turn)
    par_x, targets = parent(got, given, side, u.reshape(1), base[0, :16], side // 2 * cols)
    near = spread(targets, (0, 1), 2).reshape(side // 2, parents, block_rows, width)
    folded = fold(leaf_inv, leaf_off, par_x)
    near, base, folded, x_out = lax.optimization_barrier(
        (near, base, folded, lax.ppermute(par_x, both, turn))
    )
    base = base.reshape(by_block)

    mine = jnp.where(u < 2, near[:1], near[1:])
    near_other = lax.ppermute(near, "row", swap)
    far = [along(mine, -1), along(mine, 1)]

    half = backward(flat, near_places, base, folded, [near, near_other])
    far, half = lax.optimization_barrier((far, half))
    far_other = [lax.ppermute(a, "row", swap) for a in far]
    leaf_x = backward(flat, far_places, base, folded, far + far_other, half)
    return (leaf_x.reshape(leaf_rhs.shape), x_out)


def solution(mesh):
    rows, cols = mesh.shape["row"], mesh.shape["col"]
    return jax.shard_map(
        functools.partial(on_device, rows, cols),
        mesh=mesh,
        in_specs=(
            P(("row", "col"), None, None),
            P(("row", "col"), None, None),
            P(("row", "col"), None, None, None),
            P(("row", "col"), None),
            P("col", "row", None),
            P("col", "row", None),
        ),
        out_specs=(P(("row", "col"), None, None), P("col", "row", None)),
        check_vma=False,
    )
```
